32 devices in a mesh: row: 2 (over core), col: 16 (over z, y, x).
Axes of the slice: x: 2, y: 2, z: 4, core: 2. Of those that a mesh axis runs over, the one named last changes fastest.
Arguments:
- spectra: bfloat16 [2, 512, 20480], P(None, None, ('row', 'col')), may hold values from -6 to 6
Outputs:
- cross: bfloat16 [2, 20480, 20480], P(None, 'row', 'col')
The draws below stay inside these ranges and needn't reach their ends.
All inputs are finite; a program needn't handle non-finite values.
Results may differ from the reference program's by a relative error of at most 0.0049.
Values may be sent and summed in bfloat16 or wider, within the bound.
A program may use at most 256 MiB of HBM per device.

```python
import jax
import jax.numpy as jnp
from jax import lax

C = 20480
SEG = 512
N_ROW = 2


def block_scale(own_key, dims, shards, low, largest):
    gain = 1.0
    for position, parts in shards:
        steps = jax.random.uniform(jax.random.fold_in(jax.random.fold_in(own_key, 6), position), (parts,), jnp.float32, low / len(shards), largest / len(shards))
        gain = gain * jnp.repeat(jnp.exp(steps), dims[position] // parts).reshape((-1,) + (1,) * (len(dims) - 1 - position))
    return gain


def bell_draw(stream_key, dims, spread, reach, pieces=(), dtype=jnp.bfloat16):
    values = jax.random.normal(stream_key, dims, jnp.float32) * spread
    if len(pieces) > 0:
        values = block_scale(stream_key, dims, pieces, -0.22, 0.18) * values
    return jnp.clip(values, min=-reach, max=reach).astype(dtype)


def setup_inputs(seed: int = 0) -> dict:
    streams_of = jax.random.split(jax.random.key(seed), 2)
    spectra = bell_draw(streams_of[0], (2, SEG, C), 1.0, 6.0, ((2, 32),))
    return {"spectra": spectra}


def whiten(spectra):
    floats = spectra.astype(jnp.float32)
    magnitude = jnp.sqrt(floats[0] * floats[0] + floats[1] * floats[1])
    return (floats / jnp.maximum(magnitude, 1.0)).astype(jnp.bfloat16)

def reference(spectra):
    whitened = whiten(spectra).astype(jnp.float32)
    row_width = C // N_ROW
    stacked = jnp.moveaxis(whitened.reshape(2, SEG, N_ROW, row_width), 2, 0)
    highest = lax.Precision.HIGHEST

    def row_cross(row_block):
        real_part = jnp.dot(row_block[0].T, whitened[0], precision=highest) + jnp.dot(row_block[1].T, whitened[1], precision=highest)
        imag_part = jnp.dot(row_block[1].T, whitened[0], precision=highest) - jnp.dot(row_block[0].T, whitened[1], precision=highest)
        return (jnp.stack([real_part, imag_part]) / SEG).astype(jnp.bfloat16)
    results = lax.map(row_cross, stacked)
    return jnp.moveaxis(results, 0, 1).reshape(2, C, C)
```

```python
import functools

import jax
import jax.numpy as jnp
from jax import lax
from jax.experimental import pallas as pl
from jax.experimental.pallas import tpu as pltpu
from jax.sharding import PartitionSpec as P


def whiten(spectra):
    floats = spectra.astype(jnp.float32)
    magnitude = jnp.sqrt(floats[0] * floats[0] + floats[1] * floats[1])
    return (floats / jnp.maximum(magnitude, 1.0)).astype(jnp.bfloat16)


def contract(left, right):
    return lax.dot_general(
        left, right, (((0,), (0,)), ((), ())), preferred_element_type=jnp.float32
    )


def cross_products(row_block, column_panel, segments):
    real_part = contract(row_block[0], column_panel[0]) + contract(row_block[1], column_panel[1])
    imag_part = contract(row_block[1], column_panel[0]) - contract(row_block[0], column_panel[1])
    result = jnp.stack([real_part, imag_part])
    return (result / segments).astype(jnp.bfloat16)


def per_device_general(spectra):
    whitened = whiten(spectra)
    row_count = lax.axis_size("row")
    col_count = lax.axis_size("col")
    channels = spectra.shape[2] * row_count * col_count
    row_width = channels // row_count
    panel_width = channels // col_count
    row_block = lax.all_gather(whitened, "col", axis=2, tiled=True)
    first_channel = lax.axis_index("col") * panel_width
    offset = first_channel % row_width
    root_row = first_channel // row_width
    own_slice = lax.dynamic_slice_in_dim(row_block, offset, panel_width, 2)
    here = lax.axis_index("row") == root_row
    column_panel = lax.psum(jnp.where(here, own_slice, jnp.zeros_like(own_slice)), "row")
    return cross_products(row_block, column_panel, spectra.shape[1])


TILE = 256


def multiply_kernel(count, scale, owners, *refs):
    lefts = refs[: 2 * count]
    panel = refs[2 * count]
    out, held = refs[-2], refs[-1]
    segments = lefts[0].shape[1]
    step = pl.program_id(0)
    for block in range(count):

        @pl.when(step == block)
        def _():
            held[:, :segments] = lefts[2 * block][0].T
            held[:, segments:] = lefts[2 * block + 1][0].T

    for part in range(2):
        for first in range(0, out.shape[2], TILE):
            columns = slice(first, first + TILE)
            product = jnp.dot(
                held[...], panel[part, :, columns], preferred_element_type=jnp.float32
            )
            out[part, :, columns] = (product * scale).astype(out.dtype)


def multiply(total, blocks, panel, rows):
    count = len(blocks)
    segments, width = blocks[0][1][0].shape[1:]
    panel_width = panel.shape[2]
    owners = jnp.stack([jnp.asarray(owner, jnp.int32) for owner, _, _ in blocks])
    operands, specs = [], []
    for _, *parts in blocks:
        for array, index in parts:
            operands.append(array)
            specs.append(
                pl.BlockSpec(
                    (1, segments, width),
                    lambda i, owners, index=index: (index, 0, 0),
                    pipeline_mode=pl.Buffered(1),
                )
            )
    operands.append(panel)
    specs.append(
        pl.BlockSpec(panel.shape, lambda i, owners: (0, 0, 0), pipeline_mode=pl.Buffered(1))
    )
    aliases = {}
    if total is not None:
        aliases = {1 + len(operands): 0}
        operands.append(total)
        specs.append(pl.BlockSpec(memory_space=pl.ANY))
    return pl.pallas_call(
        functools.partial(multiply_kernel, count, 1.0 / segments),
        out_shape=jax.ShapeDtypeStruct((2, rows, panel_width), jnp.bfloat16),
        grid_spec=pltpu.PrefetchScalarGridSpec(
            num_scalar_prefetch=1,
            grid=(count,),
            in_specs=specs,
            out_specs=pl.BlockSpec((2, width, panel_width), lambda i, owners: (0, owners[i], 0)),
            scratch_shapes=[pltpu.VMEM((width, 2 * segments), jnp.bfloat16)],
        ),
        input_output_aliases=aliases,
        compiler_params=pltpu.CompilerParams(vmem_limit_bytes=40 * 2**20),
        cost_estimate=pl.CostEstimate(
            flops=count * 2 * width * 2 * segments * 2 * panel_width,
            bytes_accessed=count * 4 * width * (segments + panel_width) + 2 * panel.size,
            transcendentals=0,
        ),
    )(owners, *operands)


def per_device_block(spectra):
    segments, width = spectra.shape[1:]
    row_count, col_count = lax.axis_size("row"), lax.axis_size("col")
    rows = width * col_count
    devices = row_count * col_count
    core, me = lax.axis_index("row"), lax.axis_index("col")
    z = me // 4
    inner = (z == 1) | (z == 2)

    def chips(z_pairs, change):
        return [
            (a * 4 + k, b * 4 + (k ^ change)) for a, b in z_pairs for k in range(4)
        ]

    levels = [(k, k) for k in range(4)]
    x_pairs, y_pairs = chips(levels, 1), chips(levels, 2)
    near_pairs = chips([(k, k ^ 1) for k in range(4)], 0)
    middle_pairs = chips([(1, 2), (2, 1)], 0)
    end_pairs = chips([(1, 0), (2, 3)], 0)

    def send(array, pairs):
        return lax.ppermute(array, "col", pairs)

    own = whiten(spectra)

    panel_pairs = [
        (f, (f % row_count) * col_count + f // row_count) for f in range(devices)
    ]
    mine = lax.ppermute(own, ("row", "col"), panel_pairs)
    other = lax.ppermute(mine, "row", [(0, 1), (1, 0)])
    first = jnp.where(core == 0, mine, other)
    second = jnp.where(core == 0, other, mine)
    panel = jnp.concatenate([first, second], axis=2)
    panel = jnp.stack(
        [
            jnp.concatenate([panel[0], panel[1]], axis=0),
            jnp.concatenate([-panel[1], panel[0]], axis=0),
        ]
    )

    def plane(array):
        by_x, by_y = send(array, x_pairs), send(array, y_pairs)
        return by_x, by_y

    def corner(by_x, by_y):
        return send(by_x[:1], y_pairs), send(by_y[1:], x_pairs)

    def whole(array):
        return (array, 0), (array, 1)

    def halves(pair):
        return (pair[0], 0), (pair[1], 0)

    near = send(own, near_pairs)
    far_middle = send(own, middle_pairs)
    far = jnp.where(inner, far_middle, send(far_middle, end_pairs))
    last_middle = send(near, middle_pairs)
    last = jnp.where(inner, last_middle, send(last_middle, end_pairs))

    own_x, own_y = plane(own)
    own_xy = corner(own_x, own_y)
    near_x, near_y = plane(near)
    far_x, far_y = plane(far)
    last_x, last_y = plane(last)
    last_xy = corner(last_x, last_y)
    near_xy = tuple(send(part, near_pairs) for part in own_xy)
    far_xy = []
    for part in own_xy:
        middle = send(part, middle_pairs)
        far_xy.append(jnp.where(inner, middle, send(middle, end_pairs)))

    k = me % 4
    near_z = z ^ 1
    far_z = jnp.where(z < 2, 2, 1)
    last_z = jnp.where(z < 2, 3, 0)

    def owner(level, change):
        return level * 4 + (k ^ change)

    steps = [
        [(owner(z, 0), *whole(own)), (owner(z, 1), *whole(own_x)), (owner(z, 2), *whole(own_y))],
        [
            (owner(z, 3), *halves(own_xy)),
            (owner(near_z, 0), *whole(near)),
            (owner(near_z, 1), *whole(near_x)),
            (owner(near_z, 2), *whole(near_y)),
        ],
        [
            (owner(far_z, 0), *whole(far)),
            (owner(far_z, 1), *whole(far_x)),
            (owner(far_z, 2), *whole(far_y)),
            (owner(near_z, 3), *halves(near_xy)),
        ],
        [
            (owner(last_z, 0), *whole(last)),
            (owner(last_z, 1), *whole(last_x)),
            (owner(last_z, 2), *whole(last_y)),
        ],
        [(owner(far_z, 3), *halves(far_xy)), (owner(last_z, 3), *halves(last_xy))],
    ]
    total = None
    for blocks in steps:
        total = multiply(total, blocks, panel, rows)
    return total


def solution(mesh):
    in_specs = (P(None, None, ("row", "col")),)
    out_specs = P(None, "row", "col")
    fits = mesh.shape["row"] == 2 and mesh.shape["col"] == 16
    body = per_device_block if fits else per_device_general
    return jax.shard_map(
        body, mesh=mesh, in_specs=in_specs, out_specs=out_specs, check_vma=False
    )
```

```python
import functools

import jax
import jax.numpy as jnp
from jax import lax
from jax.experimental import pallas as pl
from jax.experimental.pallas import tpu as pltpu
from jax.sharding import PartitionSpec as P


def whiten(spectra):
    floats = spectra.astype(jnp.float32)
    magnitude = jnp.sqrt(floats[0] * floats[0] + floats[1] * floats[1])
    return (floats / jnp.maximum(magnitude, 1.0)).astype(jnp.bfloat16)


def contract(left, right):
    return lax.dot_general(
        left, right, (((0,), (0,)), ((), ())), preferred_element_type=jnp.float32
    )


def cross_products(row_block, column_panel, segments):
    real_part = contract(row_block[0], column_panel[0]) + contract(row_block[1], column_panel[1])
    imag_part = contract(row_block[1], column_panel[0]) - contract(row_block[0], column_panel[1])
    result = jnp.stack([real_part, imag_part])
    return (result / segments).astype(jnp.bfloat16)


def per_device_general(spectra):
    whitened = whiten(spectra)
    row_count = lax.axis_size("row")
    col_count = lax.axis_size("col")
    channels = spectra.shape[2] * row_count * col_count
    row_width = channels // row_count
    panel_width = channels // col_count
    row_block = lax.all_gather(whitened, "col", axis=2, tiled=True)
    first_channel = lax.axis_index("col") * panel_width
    offset = first_channel % row_width
    root_row = first_channel // row_width
    own_slice = lax.dynamic_slice_in_dim(row_block, offset, panel_width, 2)
    here = lax.axis_index("row") == root_row
    column_panel = lax.psum(jnp.where(here, own_slice, jnp.zeros_like(own_slice)), "row")
    return cross_products(row_block, column_panel, spectra.shape[1])


TILE = 256


def multiply_kernel(count, scale, owners, *refs):
    lefts = refs[: 2 * count]
    panel = refs[2 * count]
    out, held = refs[-2], refs[-1]
    segments = lefts[0].shape[1]
    step = pl.program_id(0)
    for block in range(count):

        @pl.when(step == block)
        def _():
            held[:, :segments] = lefts[2 * block][0].T
            held[:, segments:] = lefts[2 * block + 1][0].T

    for part in range(2):
        for first in range(0, out.shape[2], TILE):
            columns = slice(first, first + TILE)
            product = jnp.dot(
                held[...], panel[part, :, columns], preferred_element_type=jnp.float32
            )
            out[part, :, columns] = (product * scale).astype(out.dtype)


def multiply(total, blocks, panel, rows):
    count = len(blocks)
    segments, width = blocks[0][1][0].shape[1:]
    panel_width = panel.shape[2]
    owners = jnp.stack([jnp.asarray(owner, jnp.int32) for owner, _, _ in blocks])
    operands, specs = [], []
    for _, *parts in blocks:
        for array, index in parts:
            operands.append(array)
            specs.append(
                pl.BlockSpec(
                    (1, segments, width),
                    lambda i, owners, index=index: (index, 0, 0),
                    pipeline_mode=pl.Buffered(1),
                )
            )
    operands.append(panel)
    specs.append(
        pl.BlockSpec(panel.shape, lambda i, owners: (0, 0, 0), pipeline_mode=pl.Buffered(1))
    )
    aliases = {}
    if total is not None:
        aliases = {1 + len(operands): 0}
        operands.append(total)
        specs.append(pl.BlockSpec(memory_space=pl.ANY))
    return pl.pallas_call(
        functools.partial(multiply_kernel, count, 1.0 / segments),
        out_shape=jax.ShapeDtypeStruct((2, rows, panel_width), jnp.bfloat16),
        grid_spec=pltpu.PrefetchScalarGridSpec(
            num_scalar_prefetch=1,
            grid=(count,),
            in_specs=specs,
            out_specs=pl.BlockSpec((2, width, panel_width), lambda i, owners: (0, owners[i], 0)),
            scratch_shapes=[pltpu.VMEM((width, 2 * segments), jnp.bfloat16)],
        ),
        input_output_aliases=aliases,
        compiler_params=pltpu.CompilerParams(vmem_limit_bytes=40 * 2**20),
        cost_estimate=pl.CostEstimate(
            flops=count * 2 * width * 2 * segments * 2 * panel_width,
            bytes_accessed=count * 4 * width * (segments + panel_width) + 2 * panel.size,
            transcendentals=0,
        ),
    )(owners, *operands)


def per_device_block(spectra):
    segments, width = spectra.shape[1:]
    row_count, col_count = lax.axis_size("row"), lax.axis_size("col")
    rows = width * col_count
    devices = row_count * col_count
    core, me = lax.axis_index("row"), lax.axis_index("col")
    z = me // 4
    inner = (z == 1) | (z == 2)

    def chips(z_pairs, change):
        return [
            (a * 4 + k, b * 4 + (k ^ change)) for a, b in z_pairs for k in range(4)
        ]

    levels = [(k, k) for k in range(4)]
    x_pairs, y_pairs = chips(levels, 1), chips(levels, 2)
    near_pairs = chips([(k, k ^ 1) for k in range(4)], 0)
    middle_pairs = chips([(1, 2), (2, 1)], 0)
    end_pairs = chips([(1, 0), (2, 3)], 0)

    def send(array, pairs):
        return lax.ppermute(array, "col", pairs)

    own = whiten(spectra)

    panel_pairs = [
        (f, (f % row_count) * col_count + f // row_count) for f in range(devices)
    ]
    mine = lax.ppermute(own, ("row", "col"), panel_pairs)
    other = lax.ppermute(mine, "row", [(0, 1), (1, 0)])
    first = jnp.where(core == 0, mine, other)
    second = jnp.where(core == 0, other, mine)
    panel = jnp.concatenate([first, second], axis=2)
    panel = jnp.stack(
        [
            jnp.concatenate([panel[0], panel[1]], axis=0),
            jnp.concatenate([-panel[1], panel[0]], axis=0),
        ]
    )

    def plane(array):
        by_x, by_y = send(array, x_pairs), send(array, y_pairs)
        return by_x, by_y

    def corner(by_x, by_y):
        return send(by_x[:1], y_pairs), send(by_y[1:], x_pairs)

    def whole(array):
        return (array, 0), (array, 1)

    def halves(pair):
        return (pair[0], 0), (pair[1], 0)

    near = send(own, near_pairs)
    far_middle = send(own, middle_pairs)
    far = jnp.where(inner, far_middle, send(far_middle, end_pairs))
    last_middle = send(near, middle_pairs)
    last = jnp.where(inner, last_middle, send(last_middle, end_pairs))

    own_x, own_y = plane(own)
    own_xy = corner(own_x, own_y)
    near_x, near_y = plane(near)
    far_x, far_y = plane(far)
    last_x, last_y = plane(last)
    last_xy = corner(last_x, last_y)
    near_xy = tuple(send(part, near_pairs) for part in own_xy)
    far_xy = []
    for part in own_xy:
        middle = send(part, middle_pairs)
        far_xy.append(jnp.where(inner, middle, send(middle, end_pairs)))

    k = me % 4
    near_z = z ^ 1
    far_z = jnp.where(z < 2, 2, 1)
    last_z = jnp.where(z < 2, 3, 0)

    def owner(level, change):
        return level * 4 + (k ^ change)

    steps = [
        [
            (owner(z, 0), *whole(own)),
            (owner(z, 1), *whole(own_x)),
            (owner(z, 2), *whole(own_y)),
            (owner(z, 3), *halves(own_xy)),
        ],
        [
            (owner(near_z, 0), *whole(near)),
            (owner(near_z, 1), *whole(near_x)),
            (owner(near_z, 2), *whole(near_y)),
            (owner(far_z, 0), *whole(far)),
        ],
        [
            (owner(far_z, 1), *whole(far_x)),
            (owner(far_z, 2), *whole(far_y)),
            (owner(near_z, 3), *halves(near_xy)),
            (owner(last_z, 0), *whole(last)),
        ],
        [
            (owner(far_z, 3), *halves(far_xy)),
            (owner(last_z, 1), *whole(last_x)),
            (owner(last_z, 2), *whole(last_y)),
        ],
        [(owner(last_z, 3), *halves(last_xy))],
    ]
    total = None
    for blocks in steps:
        total = multiply(total, blocks, panel, rows)
    return total


def solution(mesh):
    in_specs = (P(None, None, ("row", "col")),)
    out_specs = P(None, "row", "col")
    fits = mesh.shape["row"] == 2 and mesh.shape["col"] == 16
    body = per_device_block if fits else per_device_general
    return jax.shard_map(
        body, mesh=mesh, in_specs=in_specs, out_specs=out_specs, check_vma=False
    )
```
